32 devices in a mesh: prompt: 8 (over z, y), head: 4 (over x, core).
Axes of the slice: x: 2, y: 2, z: 4, core: 2. Of those that a mesh axis runs over, the one named last changes fastest.
Arguments:
- queries: bfloat16 [8, 64, 4, 32, 128], P('prompt', None, None, 'head'), may hold values from -12 to 12
- new_keys: bfloat16 [8, 64, 4, 4, 128], P('prompt', None, None, 'head'), may hold values from -8 to 8
- new_values: bfloat16 [8, 64, 4, 4, 128], P('prompt', None, None, 'head'), may hold values from -6 to 6
- prefix_keys: bfloat16 [8, 4, 4096, 128], P('prompt', 'head'), may hold values from -6 to 6
- prefix_values: bfloat16 [8, 4, 4096, 128], P('prompt', 'head'), may hold values from -6 to 6
- suffix_keys: bfloat16 [8, 64, 4, 64, 128], P('prompt', None, 'head'), may hold values from -8 to 8
- suffix_values: bfloat16 [8, 64, 4, 64, 128], P('prompt', None, 'head'), may hold values from -6 to 6
- suffix_lengths: int32 [8, 64], P('prompt'), may hold values from 1 to 64, as said below
- sample_counts: int32 [8], P('prompt'), may hold values from 8 to 64, as said below
- out_weight: bfloat16 [4096, 8192], P('head', 'prompt'), may hold values from -0.09375 to 0.09375
Outputs:
- projected: bfloat16 [4, 512, 8192], P(None, 'head', 'prompt')
The draws below stay inside these ranges and needn't reach their ends.
Inputs may be any that keep to these rules, and one draw needn't show every extreme that they name: A sample's suffix holds its first suffix_lengths positions; some sample has 64. `sample_counts`: each count is 8, 16, 32 or 64; the samples of a prompt fill its first slots; some prompt has 64.
All inputs are finite; a program needn't handle non-finite values.
Results may differ from the reference program's by a relative error of at most 0.012.
Values may be sent and summed in bfloat16 or wider, within the bound.
A program may use at most 128 MiB of HBM per device.

```python
import jax
import jax.numpy as jnp
from jax import lax

D = 8192
HD = 128
GROUP = 8
PREFIX = 4096
SLOTS = 64
SUFFIX = 64
STEPS = 4
KVH = 4
QH = 32
PROMPTS = 8


def shared_parts(key):
    base_key = jax.random.fold_in(key, 4242)
    key_a = jax.random.fold_in(base_key, 0)
    sample_dir = jnp.clip(jax.random.normal(key_a, (PROMPTS, SLOTS, KVH, HD), jnp.float32), -3.0, 3.0)
    return sample_dir


def draw_queries(key, part):
    sample_dir = shared_parts(key)
    array_shape = (PROMPTS, SLOTS, STEPS, QH, HD)
    noise_key = jax.random.fold_in(key, 1)
    sample_along = jnp.repeat(sample_dir, GROUP, axis=2)[:, :, None]
    limit_value = 12.0 * 128.0 / HD
    noise_part = jnp.clip(jax.random.normal(noise_key, array_shape, jnp.float32), -6.0, 6.0)
    values = noise_part + 0.8 * sample_along
    return jnp.clip(values, -limit_value, limit_value).astype(jnp.bfloat16)


def draw_prefix_keys(key, part):
    array_shape = (PROMPTS, KVH, PREFIX, HD)
    noise_key = jax.random.fold_in(key, 2)
    values = jax.random.normal(noise_key, array_shape, jnp.float32)
    return jnp.clip(values, -6.0, 6.0).astype(jnp.bfloat16)


def draw_suffix_keys(key, part):
    sample_dir = shared_parts(key)
    array_shape = (PROMPTS, SLOTS, KVH, SUFFIX, HD)
    noise_key = jax.random.fold_in(key, 3)
    noise_part = jnp.clip(jax.random.normal(noise_key, array_shape, jnp.float32), -5.0, 5.0)
    return jnp.clip(noise_part + 0.5 * sample_dir[:, :, :, None, :], -8.0, 8.0).astype(jnp.bfloat16)


def draw_new_keys(key, part):
    sample_dir = shared_parts(key)
    array_shape = (PROMPTS, SLOTS, STEPS, KVH, HD)
    noise_key = jax.random.fold_in(key, 4)
    noise_part = jnp.clip(jax.random.normal(noise_key, array_shape, jnp.float32), -5.0, 5.0)
    return jnp.clip(noise_part + 0.8 * sample_dir[:, :, None], -8.0, 8.0).astype(jnp.bfloat16)


def draw_suffix_lengths(key, part):
    length_key = jax.random.fold_in(key, 5)
    lengths = jax.random.randint(length_key, (PROMPTS, SLOTS), 1, SUFFIX + 1)
    chosen = jax.random.randint(jax.random.fold_in(key, 6), (), 0, PROMPTS * SLOTS)
    flat_ids = jnp.arange(PROMPTS * SLOTS).reshape(PROMPTS, SLOTS)
    return jnp.where(flat_ids == chosen, SUFFIX, lengths).astype(jnp.int32)


def draw_sample_counts(key, part):
    power_key = jax.random.fold_in(key, 7)
    powers = jax.random.randint(power_key, (PROMPTS,), 0, 4)
    counts = SLOTS // 8 * jnp.left_shift(jnp.ones((PROMPTS,), jnp.int32), powers)
    chosen = jax.random.randint(jax.random.fold_in(key, 8), (), 0, PROMPTS)
    return jnp.where(jnp.arange(PROMPTS) == chosen, SLOTS, counts).astype(jnp.int32)


def levels(rng, dims, pieces, least, top_value):
    def one(axis_at, blocks):
        heights = jax.random.uniform(jax.random.fold_in(jax.random.fold_in(rng, 6), axis_at), (blocks,), jnp.float32, least / len(pieces), top_value / len(pieces))
        return jnp.repeat(jnp.exp(heights), dims[axis_at] // blocks).reshape((-1,) + (1,) * (len(dims) - axis_at - 1))

    level = one(*pieces[0])
    for cut in pieces[1:]:
        level = level * one(*cut)
    return level


def scatter_about(own_key, shape, spread, limit, cuts=(), kind=jnp.bfloat16):
    array = spread * jax.random.normal(own_key, shape, jnp.float32)
    if cuts:
        array = array * levels(own_key, shape, cuts, -0.22, 0.18)
    return jnp.clip(array, -limit, limit).astype(kind)


def setup_inputs(seed: int = 0) -> dict:
    seeds = jax.random.split(jax.random.key(seed), 11)
    queries = draw_queries(jax.random.fold_in(seeds[10], 71), 0)
    new_keys = draw_new_keys(jax.random.fold_in(seeds[10], 71), 0)
    new_values = scatter_about(seeds[2], (PROMPTS, SLOTS, STEPS, KVH, HD), 1.0, 6.0, ((0, 8), (3, 4)))
    prefix_keys = draw_prefix_keys(jax.random.fold_in(seeds[10], 71), 0)
    prefix_values = scatter_about(seeds[4], (PROMPTS, KVH, PREFIX, HD), 1.0, 6.0, ((0, 8), (1, 4)))
    suffix_keys = draw_suffix_keys(jax.random.fold_in(seeds[10], 71), 0)
    suffix_values = scatter_about(seeds[6], (PROMPTS, SLOTS, KVH, SUFFIX, HD), 1.0, 6.0, ((0, 8), (2, 4)))
    suffix_lengths = draw_suffix_lengths(jax.random.fold_in(seeds[10], 71), 0)
    sample_counts = draw_sample_counts(jax.random.fold_in(seeds[10], 71), 0)
    out_weight = scatter_about(seeds[9], (QH * HD, D), (QH * HD) ** -0.5, 0.09375, ((0, 4), (1, 8)))
    return {"queries": queries, "new_keys": new_keys, "new_values": new_values, "prefix_keys": prefix_keys, "prefix_values": prefix_values, "suffix_keys": suffix_keys, "suffix_values": suffix_values, "suffix_lengths": suffix_lengths, "sample_counts": sample_counts, "out_weight": out_weight}


def rounded_weights(weights):
    return lax.optimization_barrier(weights.astype(jnp.bfloat16)).astype(jnp.float32)


def attend_one(query_part, pre_keys, pre_values, tail_keys, tail_values, fresh_keys, fresh_values, tail_lengths, live_count):
    score_scale = HD ** -0.5
    query_f32 = query_part.astype(jnp.float32)
    pre_scores = jnp.einsum('stgd,kd->stgk', query_f32, pre_keys.astype(jnp.float32)) * score_scale
    tail_scores = jnp.einsum('stgd,skd->stgk', query_f32, tail_keys.astype(jnp.float32)) * score_scale
    fresh_scores = jnp.einsum('stgd,sjd->stgj', query_f32, fresh_keys.astype(jnp.float32)) * score_scale
    tail_ok = (jnp.arange(SUFFIX, dtype=jnp.int32)[None, :] < tail_lengths[:, None])[:, None, None, :]
    step_ids = jnp.arange(STEPS, dtype=jnp.int32)
    fresh_ok = (step_ids[None, :] <= step_ids[:, None])[None, :, None, :]
    tail_scores = jnp.where(tail_ok, tail_scores, -1e30)
    fresh_scores = jnp.where(fresh_ok, fresh_scores, -1e30)
    row_top = jnp.maximum(jnp.maximum(jnp.max(pre_scores, axis=-1), jnp.max(tail_scores, axis=-1)), jnp.max(fresh_scores, axis=-1))
    pre_weights = jnp.exp(pre_scores - row_top[..., None])
    tail_weights = jnp.where(tail_ok, jnp.exp(tail_scores - row_top[..., None]), 0.0)
    fresh_weights = jnp.where(fresh_ok, jnp.exp(fresh_scores - row_top[..., None]), 0.0)
    totals = jnp.sum(pre_weights, axis=-1) + jnp.sum(tail_weights, axis=-1) + jnp.sum(fresh_weights, axis=-1)
    numerator = jnp.einsum('stgk,kd->stgd', rounded_weights(pre_weights), pre_values.astype(jnp.float32))
    numerator = numerator + jnp.einsum('stgk,skd->stgd', rounded_weights(tail_weights), tail_values.astype(jnp.float32))
    numerator = numerator + jnp.einsum('stgj,sjd->stgd', rounded_weights(fresh_weights), fresh_values.astype(jnp.float32))
    mixed = numerator / totals[..., None]
    live_rows = jnp.arange(SLOTS, dtype=jnp.int32) < live_count
    return jnp.where(live_rows[:, None, None, None], mixed, 0.0).astype(jnp.bfloat16)


def reference(queries, new_keys, new_values, prefix_keys, prefix_values, suffix_keys, suffix_values, suffix_lengths, sample_counts, out_weight):
    def one_prompt(prompt_id):
        def one_head(head_id):
            query_part = lax.dynamic_slice_in_dim(queries[prompt_id], head_id * GROUP, GROUP, 2)
            return attend_one(query_part, prefix_keys[prompt_id, head_id], prefix_values[prompt_id, head_id],
                              suffix_keys[prompt_id][:, head_id], suffix_values[prompt_id][:, head_id],
                              new_keys[prompt_id][:, :, head_id], new_values[prompt_id][:, :, head_id],
                              suffix_lengths[prompt_id], sample_counts[prompt_id])
        return lax.map(one_head, jnp.arange(KVH, dtype=jnp.int32))

    gathered = lax.map(one_prompt, jnp.arange(PROMPTS, dtype=jnp.int32))
    attended = jnp.transpose(gathered, (3, 0, 2, 1, 4, 5)).reshape(STEPS, PROMPTS * SLOTS, QH * HD)
    results = []
    for step_index in range(STEPS):
        results.append(jnp.dot(attended[step_index], out_weight, preferred_element_type=jnp.float32).astype(jnp.bfloat16))
    return jnp.stack(results, 0)
```

```python
import functools
import math

import jax
import jax.numpy as jnp
from jax import lax
from jax.experimental import pallas as pl
from jax.experimental.pallas import tpu as pltpu
from jax.sharding import PartitionSpec as P

NEG = -1e30
SAMPLES = 16
GROUPED = 4


def attend_chunk(
    first, q_ref, key_ref, val_ref, tk_ref, tv_ref, nk_ref, nv_ref, bias_ref, live_ref,
    score_ref, mixed_ref, steps, group,
):
    hd = q_ref.shape[1]
    per = steps * group
    rows = SAMPLES * per
    suffix = tk_ref.shape[0] * per // q_ref.shape[0]
    scale = (hd ** -0.5) * math.log2(math.e)
    nt = (((1,), (1,)), ((), ()))
    f32 = jnp.float32
    prefix = key_ref.shape[0]
    tile = 512
    sub = GROUPED * per
    q = q_ref[pl.ds(pl.multiple_of(first * per, rows), rows), :]
    top = None
    for k in range(prefix // tile):
        s = lax.dot_general(q, key_ref[k * tile:(k + 1) * tile, :], nt, preferred_element_type=f32)
        score_ref[:, k * tile:(k + 1) * tile] = s
        for c in range(tile // 128):
            piece = s[:, c * 128:(c + 1) * 128]
            top = piece if top is None else jnp.maximum(top, piece)
    row_top = jnp.max(top, axis=1, keepdims=True)
    nk = nk_ref[pl.ds(pl.multiple_of(first * steps, SAMPLES * steps), SAMPLES * steps), :]
    nv = nv_ref[pl.ds(pl.multiple_of(first * steps, SAMPLES * steps), SAMPLES * steps), :]
    ns = lax.dot_general(q, nk, nt, preferred_element_type=f32)
    r = lax.broadcasted_iota(jnp.int32, ns.shape, 0)
    j = lax.broadcasted_iota(jnp.int32, ns.shape, 1)
    ok = (j // steps == r // per) & (j % steps <= (r % per) // group)
    ns = jnp.where(ok, ns, NEG)
    row_top = jnp.maximum(row_top, jnp.max(ns, axis=1, keepdims=True))
    width = GROUPED * suffix
    tails = []
    for g in range(SAMPLES // GROUPED):
        at = pl.multiple_of((first + g * GROUPED) * suffix, width)
        ts = lax.dot_general(q[g * sub:(g + 1) * sub], tk_ref[pl.ds(at, width), :], nt, preferred_element_type=f32)
        r = lax.broadcasted_iota(jnp.int32, ts.shape, 0)
        j = lax.broadcasted_iota(jnp.int32, ts.shape, 1)
        ts = jnp.where(j // suffix == r // per, ts + bias_ref[:, pl.ds(at, width)], NEG)
        tails.append(ts)
    tail = jnp.concatenate(tails, axis=0)
    row_top = jnp.maximum(row_top, jnp.max(tail, axis=1, keepdims=True))
    nw = jnp.exp2((ns - row_top) * scale)
    tw = jnp.exp2((tail - row_top) * scale)
    total = jnp.sum(nw, axis=1, keepdims=True) + jnp.sum(tw, axis=1, keepdims=True)
    numer = jnp.dot(nw.astype(jnp.bfloat16), nv, preferred_element_type=f32)
    tw = tw.astype(jnp.bfloat16)
    parts = []
    for g in range(SAMPLES // GROUPED):
        at = pl.multiple_of((first + g * GROUPED) * suffix, width)
        parts.append(jnp.dot(tw[g * sub:(g + 1) * sub], tv_ref[pl.ds(at, width), :], preferred_element_type=f32))
    numer = numer + jnp.concatenate(parts, axis=0)
    wide = None
    for k in range(prefix // tile):
        w = jnp.exp2((score_ref[:, k * tile:(k + 1) * tile] - row_top) * scale).astype(jnp.bfloat16)
        d = jnp.dot(w, val_ref[k * tile:(k + 1) * tile, :], preferred_element_type=f32)
        wide = d if wide is None else wide + d
    numer = numer + wide[:, :hd]
    total = total + wide[:, hd:hd + 1]
    mixed = numer / total
    live = live_ref[pl.ds(pl.multiple_of(first * per, rows), rows), :]
    mixed_ref[...] = jnp.where(live > 0.0, mixed, 0.0)


def place_chunk(mixed_ref, out_ref, row, first, steps, group, hd):
    for t in range(steps):
        for g in range(group):
            piece = mixed_ref[pl.ds(t * group + g, SAMPLES, stride=steps * group), :]
            out_ref[row + t, pl.ds(pl.multiple_of(first, SAMPLES), SAMPLES), g * hd:(g + 1) * hd] = piece.astype(jnp.bfloat16)


def widen(v_ref, val_ref):
    hd = v_ref.shape[1]
    val_ref[:, :hd] = v_ref[...]
    val_ref[:, hd:] = jnp.ones((v_ref.shape[0], hd), val_ref.dtype)


def attention_kernel(
    steps, group, q_ref, k_ref, v_ref, tk_ref, tv_ref, nk_ref, nv_ref, bias_ref, live_ref, out_ref,
    val_ref, score_ref, mixed_ref,
):
    hd = q_ref.shape[1]
    slots = q_ref.shape[0] // (steps * group)
    widen(v_ref, val_ref)

    def body(c, _):
        first = c * SAMPLES
        attend_chunk(first, q_ref, k_ref, val_ref, tk_ref, tv_ref, nk_ref, nv_ref, bias_ref, live_ref,
                     score_ref, mixed_ref, steps, group)
        place_chunk(mixed_ref, out_ref, 0, first, steps, group, hd)
        return 0

    lax.fori_loop(0, slots // SAMPLES, body, 0)


def prepare(queries, new_keys, new_values, prefix_keys, prefix_values, suffix_keys, suffix_values, suffix_lengths, sample_counts):
    _, slots, steps, group, hd = queries.shape
    suffix = suffix_keys.shape[3]
    bias = jnp.where(lax.broadcasted_iota(jnp.int32, (slots, suffix), 1) < suffix_lengths[0][:, None], 0.0, NEG)
    bias = bias.astype(jnp.float32).reshape(1, slots * suffix)
    per = steps * group
    live = (lax.broadcasted_iota(jnp.int32, (slots * per, hd), 0) // per < sample_counts[0]).astype(jnp.float32)
    return (
        queries.reshape(slots * per, hd),
        prefix_keys[0, 0], prefix_values[0, 0],
        suffix_keys.reshape(slots * suffix, hd), suffix_values.reshape(slots * suffix, hd),
        new_keys.reshape(slots * steps, hd), new_values.reshape(slots * steps, hd),
        bias, live,
    )


def per_device(
    queries, new_keys, new_values, prefix_keys, prefix_values, suffix_keys, suffix_values,
    suffix_lengths, sample_counts, out_weight,
):
    _, slots, steps, group, hd = queries.shape
    ins = prepare(queries, new_keys, new_values, prefix_keys, prefix_values, suffix_keys, suffix_values, suffix_lengths, sample_counts)
    prefix = prefix_keys.shape[2]
    stacked = pl.pallas_call(
        functools.partial(attention_kernel, steps, group),
        out_shape=jax.ShapeDtypeStruct((steps, slots, group * hd), jnp.bfloat16),
        in_specs=[pl.BlockSpec(memory_space=pltpu.VMEM)] * 9,
        out_specs=pl.BlockSpec(memory_space=pltpu.VMEM),
        scratch_shapes=[
            pltpu.VMEM((prefix, 2 * hd), jnp.bfloat16),
            pltpu.VMEM((SAMPLES * steps * group, prefix), jnp.float32),
            pltpu.VMEM((SAMPLES * steps * group, hd), jnp.float32),
        ],
        compiler_params=pltpu.CompilerParams(vmem_limit_bytes=48 * 2**20),
    )(*ins)
    partial_out = jnp.dot(
        lax.all_gather(stacked, "prompt", axis=1, tiled=True), out_weight, preferred_element_type=jnp.float32
    )
    return lax.psum_scatter(partial_out.astype(jnp.bfloat16), "head", scatter_dimension=1, tiled=True)


def solution(mesh):
    return jax.shard_map(
        per_device,
        mesh=mesh,
        in_specs=(
            P("prompt", None, None, "head", None),
            P("prompt", None, None, "head", None),
            P("prompt", None, None, "head", None),
            P("prompt", "head", None, None),
            P("prompt", "head", None, None),
            P("prompt", None, "head", None, None),
            P("prompt", None, "head", None, None),
            P("prompt", None),
            P("prompt"),
            P("head", "prompt"),
        ),
        out_specs=P(None, "head", "prompt"),
        check_vma=False,
    )
```

```python
import functools
import math

import jax
import jax.numpy as jnp
from jax import lax
from jax.experimental import pallas as pl
from jax.experimental.pallas import tpu as pltpu
from jax.sharding import PartitionSpec as P

NEG = -1e30
SAMPLES = 16
GROUPED = 4


def attend_chunk(
    first, q_ref, key_ref, val_ref, tk_ref, tv_ref, nk_ref, nv_ref, bias_ref, count_ref,
    score_ref, mixed_ref, steps, group,
):
    hd = q_ref.shape[1]
    per = steps * group
    rows = SAMPLES * per
    suffix = tk_ref.shape[0] * per // q_ref.shape[0]
    scale = (hd ** -0.5) * math.log2(math.e)
    nt = (((1,), (1,)), ((), ()))
    f32 = jnp.float32
    prefix = key_ref.shape[0]
    tile = 512
    sub = GROUPED * per
    q = q_ref[pl.ds(pl.multiple_of(first * per, rows), rows), :]
    top = None
    for k in range(prefix // tile):
        s = lax.dot_general(q, key_ref[k * tile:(k + 1) * tile, :], nt, preferred_element_type=f32)
        score_ref[:, k * tile:(k + 1) * tile] = s
        for c in range(tile // 128):
            piece = s[:, c * 128:(c + 1) * 128]
            top = piece if top is None else jnp.maximum(top, piece)
    row_top = jnp.max(top, axis=1, keepdims=True)
    nk = nk_ref[pl.ds(pl.multiple_of(first * steps, SAMPLES * steps), SAMPLES * steps), :]
    nv = nv_ref[pl.ds(pl.multiple_of(first * steps, SAMPLES * steps), SAMPLES * steps), :]
    ns = lax.dot_general(q, nk, nt, preferred_element_type=f32)
    r = lax.broadcasted_iota(jnp.int32, ns.shape, 0)
    j = lax.broadcasted_iota(jnp.int32, ns.shape, 1)
    ok = (j // steps == r // per) & (j % steps <= (r % per) // group)
    ns = jnp.where(ok, ns, NEG)
    row_top = jnp.maximum(row_top, jnp.max(ns, axis=1, keepdims=True))
    width = GROUPED * suffix
    tails = []
    for g in range(SAMPLES // GROUPED):
        at = pl.multiple_of((first + g * GROUPED) * suffix, width)
        ts = lax.dot_general(q[g * sub:(g + 1) * sub], tk_ref[pl.ds(at, width), :], nt, preferred_element_type=f32)
        r = lax.broadcasted_iota(jnp.int32, ts.shape, 0)
        j = lax.broadcasted_iota(jnp.int32, ts.shape, 1)
        ts = jnp.where(j // suffix == r // per, ts + bias_ref[:, pl.ds(at, width)], NEG)
        tails.append(ts)
    tail = jnp.concatenate(tails, axis=0)
    row_top = jnp.maximum(row_top, jnp.max(tail, axis=1, keepdims=True))
    nw = jnp.exp2((ns - row_top) * scale)
    tw = jnp.exp2((tail - row_top) * scale)
    total = jnp.sum(nw, axis=1, keepdims=True) + jnp.sum(tw, axis=1, keepdims=True)
    numer = jnp.dot(nw.astype(jnp.bfloat16), nv, preferred_element_type=f32)
    tw = tw.astype(jnp.bfloat16)
    parts = []
    for g in range(SAMPLES // GROUPED):
        at = pl.multiple_of((first + g * GROUPED) * suffix, width)
        parts.append(jnp.dot(tw[g * sub:(g + 1) * sub], tv_ref[pl.ds(at, width), :], preferred_element_type=f32))
    numer = numer + jnp.concatenate(parts, axis=0)
    wide = None
    for k in range(prefix // tile):
        w = jnp.exp2((score_ref[:, k * tile:(k + 1) * tile] - row_top) * scale).astype(jnp.bfloat16)
        d = jnp.dot(w, val_ref[k * tile:(k + 1) * tile, :], preferred_element_type=f32)
        wide = d if wide is None else wide + d
    numer = numer + wide[:, :hd]
    total = total + wide[:, hd:hd + 1]
    mixed = numer / total
    sample = first + lax.broadcasted_iota(jnp.int32, mixed.shape, 0) // per
    mixed_ref[...] = jnp.where(sample < count_ref[0], mixed, 0.0)


def place_chunk(mixed_ref, out_ref, row, first, steps, group, hd):
    for t in range(steps):
        for g in range(group):
            piece = mixed_ref[pl.ds(t * group + g, SAMPLES, stride=steps * group), :]
            out_ref[row + t, pl.ds(pl.multiple_of(first, SAMPLES), SAMPLES), g * hd:(g + 1) * hd] = piece.astype(jnp.bfloat16)


def widen(v_ref, val_ref):
    hd = v_ref.shape[1]
    val_ref[:, :hd] = v_ref[...]
    val_ref[:, hd:] = jnp.ones((v_ref.shape[0], hd), val_ref.dtype)


def attention_kernel(
    steps, group, q_ref, k_ref, v_ref, tk_ref, tv_ref, nk_ref, nv_ref, bias_ref, count_ref, out_ref,
    val_ref, score_ref, mixed_ref,
):
    hd = q_ref.shape[1]
    slots = q_ref.shape[0] // (steps * group)
    widen(v_ref, val_ref)

    def body(c, _):
        first = c * SAMPLES
        attend_chunk(first, q_ref, k_ref, val_ref, tk_ref, tv_ref, nk_ref, nv_ref, bias_ref, count_ref,
                     score_ref, mixed_ref, steps, group)
        place_chunk(mixed_ref, out_ref, 0, first, steps, group, hd)
        return 0

    lax.fori_loop(0, slots // SAMPLES, body, 0)


def prepare(queries, new_keys, new_values, prefix_keys, prefix_values, suffix_keys, suffix_values, suffix_lengths, sample_counts):
    _, slots, steps, group, hd = queries.shape
    suffix = suffix_keys.shape[3]
    bias = jnp.where(lax.broadcasted_iota(jnp.int32, (slots, suffix), 1) < suffix_lengths[0][:, None], 0.0, NEG)
    bias = bias.astype(jnp.float32).reshape(1, slots * suffix)
    return (
        queries.reshape(slots * steps * group, hd),
        prefix_keys[0, 0], prefix_values[0, 0],
        suffix_keys.reshape(slots * suffix, hd), suffix_values.reshape(slots * suffix, hd),
        new_keys.reshape(slots * steps, hd), new_values.reshape(slots * steps, hd),
        bias, sample_counts,
    )


def project_kernel(
    ring, heads, x_ref, w_ref, out_ref, held, sent, own, landed,
    hop_send, hop_recv, sum_send, sum_recv,
):
    steps, slots, depth = x_ref.shape
    half = steps // 2
    share = ring // heads
    cols = w_ref.shape[1]
    me = lax.axis_index("prompt")
    head = lax.axis_index("head")
    mesh_id = pl.DeviceIdType.MESH

    def prompt_at(spot):
        spot = lax.rem(spot + 2 * ring, ring)
        return jnp.where(spot < ring // 2, 2 * spot, 2 * (ring - 1 - spot) + 1)

    spot = jnp.where(lax.rem(me, 2) == 0, me // 2, ring - 1 - me // 2)
    right, left = prompt_at(spot + 1), prompt_at(spot - 1)

    barrier = pltpu.get_barrier_semaphore()
    for other in (left, right):
        pl.semaphore_signal(barrier, inc=1, device_id=(other, head), device_id_type=mesh_id)
    for d in range(1, heads):
        pl.semaphore_signal(barrier, inc=1, device_id=(me, lax.rem(head + d, heads)), device_id_type=mesh_id)
    pl.semaphore_wait(barrier, 1 + heads)

    def hop(k, t):
        return pltpu.make_async_remote_copy(
            src_ref=held.at[k - 1, t], dst_ref=held.at[k, t],
            send_sem=hop_send.at[k - 1, t], recv_sem=hop_recv.at[k - 1, t],
            device_id=(right if t < half else left, head), device_id_type=mesh_id,
        )

    def spread(k, side, source, target, prompt):
        at = lax.rem(prompt, share)
        return pltpu.make_async_remote_copy(
            src_ref=sent.at[k, side],
            dst_ref=landed.at[source, at, side],
            send_sem=sum_send.at[k, side], recv_sem=sum_recv.at[source, at, side],
            device_id=(me, target), device_id_type=mesh_id,
        )

    def prompt_of(k, side):
        return prompt_at(spot - k if side == 0 else spot + k)

    held[0] = x_ref[...]
    for t in range(steps):
        hop(1, t).start()

    def step(k, _):
        @pl.when(k > 0)
        def _():
            for t in (0, half, 1, half + 1) if steps == 4 else range(steps):
                hop(k, t).wait_recv()

                @pl.when(k < ring - 1)
                def _():
                    hop(k + 1, t).start()

        block = held[k].reshape(steps * slots, depth)
        y = jnp.dot(block, w_ref[...], preferred_element_type=jnp.float32)
        for side in range(2):
            prompt = prompt_of(k, side)
            target = prompt // share
            rows = y[side * half * slots:(side + 1) * half * slots].reshape(half, slots, cols)

            @pl.when(target == head)
            def _():
                own[lax.rem(prompt, share), side] = rows

            @pl.when(target != head)
            def _():
                sent[k, side] = rows.astype(jnp.bfloat16)
                spread(k, side, head, target, prompt).start()
        return 0

    lax.fori_loop(0, ring, step, 0)

    def drain(k, _):
        for side in range(2):
            prompt = prompt_of(k, side)
            target = prompt // share

            @pl.when(target != head)
            def _():
                spread(k, side, head, target, prompt).wait_send()

        @pl.when(k > 0)
        def _():
            for t in range(steps):
                hop(k, t).wait_send()
        return 0

    def finish(at, _):
        for side in range(2):
            for d in range(1, heads):
                source = lax.rem(head + d, heads)
                pltpu.make_async_remote_copy(
                    src_ref=sent.at[0, side], dst_ref=landed.at[source, at, side],
                    send_sem=sum_send.at[0, side], recv_sem=sum_recv.at[source, at, side],
                    device_id=(me, source), device_id_type=mesh_id,
                ).wait_recv()
            for t in range(half):
                total = own[at, side, t]
                for d in range(1, heads):
                    total = total + landed[lax.rem(head + d, heads), at, side, t].astype(jnp.float32)
                out_ref[side * half + t, pl.ds(pl.multiple_of(at * slots, slots), slots), :] = total.astype(out_ref.dtype)
        return 0

    lax.fori_loop(0, share, finish, 0)
    lax.fori_loop(0, ring, drain, 0)


def project(stacked, out_weight, ring, heads):
    steps, slots, depth = stacked.shape
    cols = out_weight.shape[1]
    half, share = steps // 2, ring // heads
    return pl.pallas_call(
        functools.partial(project_kernel, ring, heads),
        out_shape=jax.ShapeDtypeStruct((steps, share * slots, cols), jnp.bfloat16),
        in_specs=[pl.BlockSpec(memory_space=pltpu.VMEM)] * 2,
        out_specs=pl.BlockSpec(memory_space=pltpu.VMEM),
        scratch_shapes=[
            pltpu.VMEM((ring, steps, slots, depth), jnp.bfloat16),
            pltpu.VMEM((ring, 2, half, slots, cols), jnp.bfloat16),
            pltpu.VMEM((share, 2, half, slots, cols), jnp.float32),
            pltpu.VMEM((heads, share, 2, half, slots, cols), jnp.bfloat16),
            pltpu.SemaphoreType.DMA((ring, steps)),
            pltpu.SemaphoreType.DMA((ring, steps)),
            pltpu.SemaphoreType.DMA((ring, 2)),
            pltpu.SemaphoreType.DMA((heads, share, 2)),
        ],
        compiler_params=pltpu.CompilerParams(
            collective_id=0, has_side_effects=True, vmem_limit_bytes=48 * 2**20
        ),
    )(stacked, out_weight)


def per_device(
    queries, new_keys, new_values, prefix_keys, prefix_values, suffix_keys, suffix_values,
    suffix_lengths, sample_counts, out_weight, *, ring, heads,
):
    _, slots, steps, group, hd = queries.shape
    ins = prepare(queries, new_keys, new_values, prefix_keys, prefix_values, suffix_keys, suffix_values, suffix_lengths, sample_counts)
    prefix = prefix_keys.shape[2]
    stacked = pl.pallas_call(
        functools.partial(attention_kernel, steps, group),
        out_shape=jax.ShapeDtypeStruct((steps, slots, group * hd), jnp.bfloat16),
        in_specs=[pl.BlockSpec(memory_space=pltpu.VMEM)] * 8 + [pl.BlockSpec(memory_space=pltpu.SMEM)],
        out_specs=pl.BlockSpec(memory_space=pltpu.VMEM),
        scratch_shapes=[
            pltpu.VMEM((prefix, 2 * hd), jnp.bfloat16),
            pltpu.VMEM((SAMPLES * steps * group, prefix), jnp.float32),
            pltpu.VMEM((SAMPLES * steps * group, hd), jnp.float32),
        ],
        compiler_params=pltpu.CompilerParams(vmem_limit_bytes=48 * 2**20),
    )(*ins)
    return project(stacked, out_weight, ring, heads)


def solution(mesh):
    ring, heads = mesh.shape["prompt"], mesh.shape["head"]
    return jax.shard_map(
        functools.partial(per_device, ring=ring, heads=heads),
        mesh=mesh,
        in_specs=(
            P("prompt", None, None, "head", None),
            P("prompt", None, None, "head", None),
            P("prompt", None, None, "head", None),
            P("prompt", "head", None, None),
            P("prompt", "head", None, None),
            P("prompt", None, "head", None, None),
            P("prompt", None, "head", None, None),
            P("prompt", None),
            P("prompt"),
            P("head", "prompt"),
        ),
        out_specs=P(None, "head", "prompt"),
        check_vma=False,
    )
```

```python
import functools
import math

import jax
import jax.numpy as jnp
from jax import lax
from jax.experimental import pallas as pl
from jax.experimental.pallas import tpu as pltpu
from jax.sharding import PartitionSpec as P

NEG = -1e30
SAMPLES = 16
GROUPED = 4


def attend_chunk(
    first, q_ref, key_ref, val_ref, tk_ref, tv_ref, nk_ref, nv_ref, bias_ref, count_ref,
    score_ref, mixed_ref, steps, group, midway,
):
    hd = q_ref.shape[1]
    per = steps * group
    rows = SAMPLES * per
    suffix = tk_ref.shape[0] * per // q_ref.shape[0]
    scale = (hd ** -0.5) * math.log2(math.e)
    nt = (((1,), (1,)), ((), ()))
    f32 = jnp.float32
    prefix = key_ref.shape[0]
    tile = 512
    sub = GROUPED * per
    q = q_ref[pl.ds(pl.multiple_of(first * per, rows), rows), :]
    top = None
    for k in range(prefix // tile):
        s = lax.dot_general(q, key_ref[k * tile:(k + 1) * tile, :], nt, preferred_element_type=f32)
        score_ref[:, k * tile:(k + 1) * tile] = s
        for c in range(tile // 128):
            piece = s[:, c * 128:(c + 1) * 128]
            top = piece if top is None else jnp.maximum(top, piece)
    row_top = jnp.max(top, axis=1, keepdims=True)
    nk = nk_ref[pl.ds(pl.multiple_of(first * steps, SAMPLES * steps), SAMPLES * steps), :]
    nv = nv_ref[pl.ds(pl.multiple_of(first * steps, SAMPLES * steps), SAMPLES * steps), :]
    ns = lax.dot_general(q, nk, nt, preferred_element_type=f32)
    r = lax.broadcasted_iota(jnp.int32, ns.shape, 0)
    j = lax.broadcasted_iota(jnp.int32, ns.shape, 1)
    ok = (j // steps == r // per) & (j % steps <= (r % per) // group)
    ns = jnp.where(ok, ns, NEG)
    row_top = jnp.maximum(row_top, jnp.max(ns, axis=1, keepdims=True))
    width = GROUPED * suffix
    tails = []
    for g in range(SAMPLES // GROUPED):
        at = pl.multiple_of((first + g * GROUPED) * suffix, width)
        ts = lax.dot_general(q[g * sub:(g + 1) * sub], tk_ref[pl.ds(at, width), :], nt, preferred_element_type=f32)
        r = lax.broadcasted_iota(jnp.int32, ts.shape, 0)
        j = lax.broadcasted_iota(jnp.int32, ts.shape, 1)
        ts = jnp.where(j // suffix == r // per, ts + bias_ref[:, pl.ds(at, width)], NEG)
        tails.append(ts)
    tail = jnp.concatenate(tails, axis=0)
    row_top = jnp.maximum(row_top, jnp.max(tail, axis=1, keepdims=True))
    midway()
    nw = jnp.exp2((ns - row_top) * scale)
    tw = jnp.exp2((tail - row_top) * scale)
    total = jnp.sum(nw, axis=1, keepdims=True) + jnp.sum(tw, axis=1, keepdims=True)
    numer = jnp.dot(nw.astype(jnp.bfloat16), nv, preferred_element_type=f32)
    tw = tw.astype(jnp.bfloat16)
    parts = []
    for g in range(SAMPLES // GROUPED):
        at = pl.multiple_of((first + g * GROUPED) * suffix, width)
        parts.append(jnp.dot(tw[g * sub:(g + 1) * sub], tv_ref[pl.ds(at, width), :], preferred_element_type=f32))
    numer = numer + jnp.concatenate(parts, axis=0)
    wide = None
    for k in range(prefix // tile):
        w = jnp.exp2((score_ref[:, k * tile:(k + 1) * tile] - row_top) * scale).astype(jnp.bfloat16)
        d = jnp.dot(w, val_ref[k * tile:(k + 1) * tile, :], preferred_element_type=f32)
        wide = d if wide is None else wide + d
    numer = numer + wide[:, :hd]
    total = total + wide[:, hd:hd + 1]
    mixed = numer / total
    sample = first + lax.broadcasted_iota(jnp.int32, mixed.shape, 0) // per
    mixed_ref[...] = jnp.where(sample < count_ref[0], mixed, 0.0)


def place_chunk(mixed_ref, held, c, steps, group, hd):
    half = steps // 2
    for t in range(steps):
        for g in range(group):
            piece = mixed_ref[pl.ds(t * group + g, SAMPLES, stride=steps * group), :]
            held[0, t // half, c, t % half, :, g * hd:(g + 1) * hd] = piece.astype(jnp.bfloat16)


def layer_kernel(
    ring, heads, steps, group,
    q_hbm, k_hbm, v_hbm, tk_hbm, tv_hbm, w_hbm, nk_ref, nv_ref, bias_ref, count_ref, out_ref,
    q_ref, k_ref, val_ref, tk_ref, tv_ref, w_ref, score_ref, mixed_ref,
    held, keep, sent, paired, own, landed,
    in_sem, hop_send, hop_recv, sum_send, pair_recv, sum_recv,
):
    hd = q_ref.shape[1]
    chunks = held.shape[2]
    half = steps // 2
    side_rows = chunks * half * SAMPLES
    depth = held.shape[-1]
    share = ring // heads
    chips = heads // 2
    last = 2 * chunks - 1
    me = lax.axis_index("prompt")
    head = lax.axis_index("head")
    chip, core = head // 2, lax.rem(head, 2)
    sibling = 2 * chip + 1 - core
    mesh_id = pl.DeviceIdType.MESH

    val_ref[:, hd:] = jnp.ones((val_ref.shape[0], hd), val_ref.dtype)
    loads = [
        pltpu.make_async_copy(src, dst, in_sem.at[i])
        for i, (src, dst) in enumerate((
            (q_hbm, q_ref), (k_hbm, k_ref), (v_hbm, val_ref.at[:, pl.ds(0, hd)]),
            (tk_hbm, tk_ref), (tv_hbm, tv_ref), (w_hbm, w_ref),
        ))
    ]
    for load in loads:
        load.start()

    def prompt_at(spot):
        spot = lax.rem(spot + 2 * ring, ring)
        return jnp.where(spot < ring // 2, 2 * spot, 2 * (ring - 1 - spot) + 1)

    spot = jnp.where(lax.rem(me, 2) == 0, me // 2, ring - 1 - me // 2)
    right, left = prompt_at(spot + 1), prompt_at(spot - 1)

    barrier = pltpu.get_barrier_semaphore()
    for other in (left, right):
        pl.semaphore_signal(barrier, inc=1, device_id=(other, head), device_id_type=mesh_id)
    pl.semaphore_signal(barrier, inc=1, device_id=(me, sibling), device_id_type=mesh_id)
    for d in range(1, chips):
        pl.semaphore_signal(
            barrier, inc=1, device_id=(me, lax.rem(head + 2 * d, heads)), device_id_type=mesh_id
        )
    pl.semaphore_wait(barrier, 2 + chips)

    def hop(k, side, c):
        return pltpu.make_async_remote_copy(
            src_ref=held.at[k - 1, side, c], dst_ref=held.at[k, side, c],
            send_sem=hop_send.at[k - 1, side, c], recv_sem=hop_recv.at[k - 1, side, c],
            device_id=(left if side else right, head), device_id_type=mesh_id,
        )

    def pass_on(c, late):
        for older in range(chunks - 1):
            k = 2 * (c - older) - 1 + late

            @pl.when((older < c) & (k < ring - 1))
            def _():
                for side in range(2):
                    hop(k, side, older).wait_recv()
                    hop(k + 1, side, older).start()

    for load in loads[:5]:
        load.wait()

    def attend(c, _):
        attend_chunk(
            c * SAMPLES, q_ref, k_ref, val_ref, tk_ref, tv_ref, nk_ref, nv_ref, bias_ref, count_ref,
            score_ref, mixed_ref, steps, group, lambda: pass_on(c, 0),
        )
        place_chunk(mixed_ref, held, c, steps, group, hd)
        for side in range(2):
            hop(1, side, c).start()
        pass_on(c, 1)
        return 0

    lax.fori_loop(0, chunks, attend, 0)
    loads[5].wait()

    def prompt_of(k, side):
        return prompt_at(spot - k if side == 0 else spot + k)

    def to_sibling(k, side):
        return pltpu.make_async_remote_copy(
            src_ref=sent.at[k, side], dst_ref=paired.at[k, side],
            send_sem=sum_send.at[k, side], recv_sem=pair_recv.at[k, side],
            device_id=(me, sibling), device_id_type=mesh_id,
        )

    def to_holder(k, side, source, at, target):
        return pltpu.make_async_remote_copy(
            src_ref=sent.at[k, side], dst_ref=landed.at[source, at, side],
            send_sem=sum_send.at[k, side], recv_sem=sum_recv.at[source, at, side],
            device_id=(me, target), device_id_type=mesh_id,
        )

    def step(k, _):
        @pl.when(k < ring)
        def _():
            for c in range(chunks):
                @pl.when((k > 0) & ((k > last - 2 * c - 1) | (k == ring - 1)))
                def _():
                    for side in range(2):
                        hop(k, side, c).wait_recv()

                        @pl.when(k < ring - 1)
                        def _():
                            hop(k + 1, side, c).start()

            block = held[k].reshape(2 * side_rows, depth)
            y = jnp.dot(block, w_ref[...], preferred_element_type=jnp.float32)
            for side in range(2):
                target = prompt_of(k, side) // share
                rows = y[side * side_rows:(side + 1) * side_rows]

                @pl.when(lax.rem(target, 2) == core)
                def _():
                    keep[k, side] = rows

                @pl.when(lax.rem(target, 2) != core)
                def _():
                    sent[k, side] = rows.astype(jnp.bfloat16)
                    to_sibling(k, side).start()

        @pl.when(k > 0)
        def _():
            for side in range(2):
                prompt = prompt_of(k - 1, side)
                target = prompt // share
                at = lax.rem(prompt, share)

                @pl.when(lax.rem(target, 2) == core)
                def _():
                    to_sibling(k - 1, side).wait_recv()
                    both = keep[k - 1, side] + paired[k - 1, side].astype(jnp.float32)

                    @pl.when(target == head)
                    def _():
                        own[at, side] = both

                    @pl.when(target != head)
                    def _():
                        sent[k - 1, side] = both.astype(jnp.bfloat16)
                        to_holder(k - 1, side, chip, at, target).start()
        return 0

    lax.fori_loop(0, ring + 1, step, 0)

    def finish(at, _):
        for side in range(2):
            for d in range(1, chips):
                source = lax.rem(chip + d, chips)
                to_holder(0, side, source, at, 2 * source + core).wait_recv()
            total = own[at, side]
            for d in range(1, chips):
                total = total + landed[lax.rem(chip + d, chips), at, side].astype(jnp.float32)
            total = total.astype(out_ref.dtype)
            for c in range(chunks):
                for t in range(half):
                    row = (c * half + t) * SAMPLES
                    to = pl.multiple_of((at * chunks + c) * SAMPLES, SAMPLES)
                    out_ref[side * half + t, pl.ds(to, SAMPLES), :] = total[row:row + SAMPLES]
        return 0

    lax.fori_loop(0, share, finish, 0)

    def drain(k, _):
        for side in range(2):
            @pl.when(prompt_of(k, side) // share != head)
            def _():
                to_sibling(k, side).wait_send()

            @pl.when(k > 0)
            def _():
                for c in range(chunks):
                    hop(k, side, c).wait_send()
        return 0

    lax.fori_loop(0, ring, drain, 0)


def per_device(
    queries, new_keys, new_values, prefix_keys, prefix_values, suffix_keys, suffix_values,
    suffix_lengths, sample_counts, out_weight, *, ring, heads,
):
    _, slots, steps, group, hd = queries.shape
    suffix = suffix_keys.shape[3]
    prefix = prefix_keys.shape[2]
    bias = jnp.where(lax.broadcasted_iota(jnp.int32, (slots, suffix), 1) < suffix_lengths[0][:, None], 0.0, NEG)
    bias = bias.astype(jnp.float32).reshape(1, slots * suffix)
    rows, depth = slots * steps * group, group * hd
    cols = out_weight.shape[1]
    half, share, chips, chunks = steps // 2, ring // heads, heads // 2, slots // SAMPLES
    side = chunks * half * SAMPLES
    hbm = pl.BlockSpec(memory_space=pltpu.HBM)
    vmem = pl.BlockSpec(memory_space=pltpu.VMEM)
    bf16, f32 = jnp.bfloat16, jnp.float32
    dma = pltpu.SemaphoreType.DMA
    return pl.pallas_call(
        functools.partial(layer_kernel, ring, heads, steps, group),
        out_shape=jax.ShapeDtypeStruct((steps, share * slots, cols), bf16),
        in_specs=[hbm] * 6 + [vmem] * 3 + [pl.BlockSpec(memory_space=pltpu.SMEM)],
        out_specs=vmem,
        scratch_shapes=[
            pltpu.VMEM((rows, hd), bf16),
            pltpu.VMEM((prefix, hd), bf16),
            pltpu.VMEM((prefix, 2 * hd), bf16),
            pltpu.VMEM((slots * suffix, hd), bf16),
            pltpu.VMEM((slots * suffix, hd), bf16),
            pltpu.VMEM((depth, cols), bf16),
            pltpu.VMEM((SAMPLES * steps * group, prefix), f32),
            pltpu.VMEM((SAMPLES * steps * group, hd), f32),
            pltpu.VMEM((ring, 2, chunks, half, SAMPLES, depth), bf16),
            pltpu.VMEM((ring, 2, side, cols), f32),
            pltpu.VMEM((ring, 2, side, cols), bf16),
            pltpu.VMEM((ring, 2, side, cols), bf16),
            pltpu.VMEM((share, 2, side, cols), f32),
            pltpu.VMEM((chips, share, 2, side, cols), bf16),
            dma((6,)),
            dma((ring, 2, chunks)),
            dma((ring, 2, chunks)),
            dma((ring, 2)),
            dma((ring, 2)),
            dma((chips, share, 2)),
        ],
        compiler_params=pltpu.CompilerParams(
            collective_id=0, has_side_effects=True, vmem_limit_bytes=58 * 2**20
        ),
    )(
        queries.reshape(rows, hd), prefix_keys[0, 0], prefix_values[0, 0],
        suffix_keys.reshape(slots * suffix, hd), suffix_values.reshape(slots * suffix, hd), out_weight,
        new_keys.reshape(slots * steps, hd), new_values.reshape(slots * steps, hd), bias, sample_counts,
    )


def solution(mesh):
    ring, heads = mesh.shape["prompt"], mesh.shape["head"]
    return jax.shard_map(
        functools.partial(per_device, ring=ring, heads=heads),
        mesh=mesh,
        in_specs=(
            P("prompt", None, None, "head", None),
            P("prompt", None, None, "head", None),
            P("prompt", None, None, "head", None),
            P("prompt", "head", None, None),
            P("prompt", "head", None, None),
            P("prompt", None, "head", None, None),
            P("prompt", None, "head", None, None),
            P("prompt", None),
            P("prompt"),
            P("head", "prompt"),
        ),
        out_specs=P(None, "head", "prompt"),
        check_vma=False,
    )
```
